32 devices in a mesh: dap: 32 (over z, y, x, core), rep: 1.
Axes of the slice: x: 2, y: 2, z: 4, core: 2. Of those that a mesh axis runs over, the one named last changes fastest.
Arguments:
- pair_rep: bfloat16 [640, 640, 128], P(('rep', 'dap')), may hold values from -6 to 6
- token_mask: int32 [640], P('rep'), may hold values 0 or 1
- norm_gain: float32 [128], replicated, may hold values from 0.1 to 1.9
- norm_bias: float32 [128], replicated, may hold values from -1.5 to 1.5
- w_query: bfloat16 [128, 128], replicated, may hold values from -1 to 1
- w_key: bfloat16 [128, 128], replicated, may hold values from -0.5 to 0.5
- w_value: bfloat16 [128, 128], replicated, may hold values from -0.5 to 0.5
- w_gate: bfloat16 [128, 128], replicated, may hold values from -0.5 to 0.5
- gate_bias: float32 [128], replicated, may hold values from -4 to 4
- w_bias: bfloat16 [128, 4], replicated, may hold values from -0.5 to 0.5
- w_out: bfloat16 [128, 128], replicated, may hold values from -1.5 to 1.5
Outputs:
- update: bfloat16 [640, 640, 128], P(('rep', 'dap'))
The draws below stay inside these ranges and needn't reach their ends.
Inputs may be any that keep to these rules, and one draw needn't show every extreme that they name: `token_mask`: 1 marks a valid token, 0 a padding token.
All inputs are finite; a program needn't handle non-finite values.
Results may differ from the reference program's by a relative error of at most 0.012.
Values may be sent and summed in bfloat16 or wider, within the bound.
A program may use at most 128 MiB of HBM per device.

```python
import jax
import jax.numpy as jnp
from jax import lax

C = 128
H = 4
DH = 32
CROP = 640
HD = 128


def with_ends(values, key, least, top_value):
    shape = values.shape
    index_at = [jax.random.randint(jax.random.fold_in(key, axis), (), 0, shape[axis]) for axis in range(len(shape))]
    values = values.at[tuple(index_at)].set(least)
    longest = shape.index(max(shape))
    index_at[longest] = (index_at[longest] + 1) % shape[longest]
    return values.at[tuple(index_at)].set(top_value)


def level_of(rng, shape, cuts, low, high):
    def one(position, parts):
        heights = jax.random.uniform(jax.random.fold_in(jax.random.fold_in(rng, 6), position), (parts,), jnp.float32, low / len(cuts), high / len(cuts))
        return jnp.repeat(jnp.exp(heights), shape[position] // parts).reshape((-1,) + (1,) * (len(shape) - position - 1))

    loudness = one(*cuts[0])
    for cut in cuts[1:]:
        loudness = loudness * one(*cut)
    return loudness


def scatter_about(key, extent, deviation, most, cuts=(), held_as=jnp.bfloat16):
    values = jax.random.normal(key, extent, jnp.float32) * deviation
    if len(cuts) > 0:
        values = level_of(key, extent, cuts, -0.22, 0.18) * values
    return jnp.clip(values, min=-most, max=most).astype(held_as)


def setup_inputs(seed: int = 0, part: int = 0) -> dict:
    key_list = jax.random.split(jax.random.key(seed), 12)
    part_keys = jax.random.split(jax.random.fold_in(key_list[11], part), 12)
    return {
        "pair_rep": scatter_about(part_keys[0], (CROP, CROP, C), 1.0, 6.0, ((0, 32),)),
        "token_mask": with_ends((jax.random.randint(part_keys[1], (CROP,), 0, 8) < 7).astype(jnp.int32), jax.random.fold_in(part_keys[1], 1), 0, 1),
        "norm_gain": jnp.clip(1.0 + 0.18 * jax.random.normal(key_list[2], (C,), jnp.float32), 0.1, 1.9),
        "norm_bias": scatter_about(key_list[3], (C,), 0.3, 1.5, (), jnp.float32),
        "w_query": scatter_about(key_list[4], (C, HD), (C // 4) ** -0.5, 1.0),
        "w_key": scatter_about(key_list[5], (C, HD), C ** -0.5, 0.5),
        "w_value": scatter_about(key_list[6], (C, HD), C ** -0.5, 0.5),
        "w_gate": scatter_about(key_list[7], (C, HD), C ** -0.5, 0.5),
        "gate_bias": scatter_about(key_list[8], (HD,), 1.0, 4.0, (), jnp.float32),
        "w_bias": scatter_about(key_list[9], (C, H), C ** -0.5, 0.5),
        "w_out": scatter_about(key_list[10], (HD, C), (HD // 8) ** -0.5, 1.5),
    }


def normalize(block, norm_gain, norm_bias):
    widened = block.astype(jnp.float32)
    average = lax.optimization_barrier(jnp.mean(widened, axis=-1, keepdims=True))
    centred = widened - average
    variance = lax.optimization_barrier(jnp.mean(centred * centred, axis=-1, keepdims=True))
    return (centred * lax.rsqrt(variance + 1e-05) * norm_gain + norm_bias).astype(jnp.bfloat16)

def attend_column(column_inputs, bias_full, key_valid, head_count):
    query_col, key_col, value_col, gate_col, col_valid = column_inputs
    crop_len = query_col.shape[0]
    query_heads = query_col.astype(jnp.float32).reshape(crop_len, head_count, -1)
    key_heads = key_col.astype(jnp.float32).reshape(crop_len, head_count, -1)
    value_heads = value_col.astype(jnp.float32).reshape(crop_len, head_count, -1)
    scores = jnp.einsum('ihd,khd->hik', query_heads, key_heads) + bias_full.astype(jnp.float32)
    allowed = key_valid * col_valid > 0
    scores = jnp.where(allowed[None, None, :], scores, -1000000000.0)
    largest = lax.optimization_barrier(jnp.max(scores, axis=-1, keepdims=True))
    weights = jnp.exp(scores - largest)
    attn_probs = (weights / lax.optimization_barrier(jnp.sum(weights, axis=-1, keepdims=True))).astype(jnp.bfloat16)
    mixed_out = jnp.einsum('hik,khd->ihd', attn_probs.astype(jnp.float32), value_heads).reshape(crop_len, -1)
    return (mixed_out * gate_col.astype(jnp.float32)).astype(jnp.bfloat16)

def reference(pair_rep, token_mask, norm_gain, norm_bias, w_query, w_key, w_value, w_gate, gate_bias, w_bias, w_out):
    normed = normalize(pair_rep, norm_gain, norm_bias)
    q_scale = DH ** (-0.5)
    query_proj = (jnp.dot(normed, w_query, preferred_element_type=jnp.float32) * q_scale).astype(jnp.bfloat16)
    key_proj = jnp.dot(normed, w_key, preferred_element_type=jnp.float32).astype(jnp.bfloat16)
    value_proj = jnp.dot(normed, w_value, preferred_element_type=jnp.float32).astype(jnp.bfloat16)
    gate_proj = jax.nn.sigmoid(jnp.dot(normed, w_gate, preferred_element_type=jnp.float32) + gate_bias).astype(jnp.bfloat16)
    bias_proj = jnp.dot(normed, w_bias, preferred_element_type=jnp.float32).astype(jnp.bfloat16)
    bias_full = jnp.transpose(bias_proj, (2, 1, 0))

    def one_column(column_inputs):
        return attend_column(column_inputs, bias_full, token_mask, H)
    gated_out = lax.map(one_column, (jnp.transpose(query_proj, (1, 0, 2)), jnp.transpose(key_proj, (1, 0, 2)), jnp.transpose(value_proj, (1, 0, 2)), jnp.transpose(gate_proj, (1, 0, 2)), token_mask))
    gated_out = jnp.transpose(gated_out, (1, 0, 2))
    return jnp.dot(gated_out, w_out, preferred_element_type=jnp.float32).astype(jnp.bfloat16)
```

```python
import functools

import jax
import jax.numpy as jnp
from jax import lax
from jax.experimental import pallas as pl
from jax.experimental.pallas import tpu as pltpu
from jax.sharding import PartitionSpec as P

LOG2E = 1.4426950408889634
TILE = 256
SAFE = 70.0
BIG = 1e30


def normalize(block, norm_gain, norm_bias):
    widened = block.astype(jnp.float32)
    average = jnp.mean(widened, axis=-1, keepdims=True)
    centred = widened - average
    variance = jnp.mean(centred * centred, axis=-1, keepdims=True)
    return (centred * lax.rsqrt(variance + 1e-05) * norm_gain + norm_bias).astype(jnp.bfloat16)


def attend_kernel(
    heads,
    head_dim,
    q_scale,
    chunk,
    mask_ref,
    x_ref,
    gain_ref,
    nbias_ref,
    wq_ref,
    wqt_ref,
    wkt_ref,
    wv_ref,
    wg_ref,
    gbias_ref,
    wo_ref,
    bias_ref,
    kmask_ref,
    live_ref,
    out_ref,
    npad,
    q_buf,
    gate_buf,
    right,
    vext,
    probs,
    top_bias,
):
    step = pl.program_id(0)
    crop = x_ref.shape[1]
    slots = npad.shape[0]
    tiles = slots // TILE
    per = TILE - head_dim
    f32, bf16 = jnp.float32, jnp.bfloat16

    @pl.when(step == 0)
    def _():
        npad[...] = jnp.zeros_like(npad)
        r = lax.broadcasted_iota(jnp.int32, (TILE, TILE), 0)
        n = lax.broadcasted_iota(jnp.int32, (TILE, TILE), 1)
        eye = jnp.where(r == n + head_dim, 1.0, 0.0).astype(bf16)
        for h in range(heads):
            for t in range(tiles):
                right[h, t] = eye
        largest = jnp.zeros((1, 1), f32)
        for h in range(heads):
            largest = jnp.maximum(
                largest, jnp.max(jnp.abs(bias_ref[h].astype(f32)), keepdims=True)
            )
        top_bias[0] = largest[0, 0]

    normed = normalize(x_ref[0], gain_ref[...], nbias_ref[...])
    for t in range(tiles):
        count = min(per, crop - t * per)
        npad[t * TILE : t * TILE + count, :] = normed[t * per : t * per + count, :]
    q_buf[...] = (
        jnp.dot(normed, wq_ref[...], preferred_element_type=f32) * q_scale
    ).astype(bf16)
    gate_buf[...] = jax.nn.sigmoid(
        jnp.dot(normed, wg_ref[...], preferred_element_type=f32) + gbias_ref[...]
    ).astype(bf16)
    nt = (((1,), (1,)), ((), ()))
    padded = npad[...]
    key_t = lax.dot_general(wkt_ref[...], padded, nt, preferred_element_type=f32).astype(bf16)
    query_t = (
        lax.dot_general(wqt_ref[...], normed, nt, preferred_element_type=f32) * q_scale
    ).astype(bf16)
    value = jnp.dot(padded, wv_ref[...], preferred_element_type=f32).astype(bf16)

    bound = jnp.zeros((1, 1), f32)
    lanes = lax.broadcasted_iota(jnp.int32, (slots, heads * head_dim), 1)
    col_on = mask_ref[step] > 0
    kept = jnp.where(col_on, kmask_ref[...].astype(f32), live_ref[...].astype(f32)).astype(bf16)
    zero = jnp.zeros_like(kept)
    value = value * kept
    for h in range(heads):
        rows = slice(h * head_dim, (h + 1) * head_dim)
        k_h = key_t[rows, :]
        q_h = query_t[rows, :]
        for t in range(tiles):
            right[h, t, 0:head_dim, :] = k_h[:, t * TILE : (t + 1) * TILE]
        k2 = jnp.max(
            jnp.sum(jnp.square(k_h.astype(f32)), axis=0, keepdims=True), axis=1, keepdims=True
        )
        q2 = jnp.max(
            jnp.sum(jnp.square(q_h.astype(f32)), axis=0, keepdims=True), axis=1, keepdims=True
        )
        bound = jnp.maximum(bound, k2 * q2)
        mine = (lanes >= h * head_dim) & (lanes < (h + 1) * head_dim)
        vext[h * slots : (h + 1) * slots, 0 : heads * head_dim] = jnp.where(mine, value, zero)
        vext[h * slots : (h + 1) * slots, heads * head_dim : 2 * heads * head_dim] = jnp.where(
            mine, kept, zero
        )
    bound = jnp.sqrt(bound[0, 0]) + top_bias[0]
    safe = bound < SAFE
    scale = jnp.where(col_on, LOG2E, 0.0)

    def scores_of(r0, h, t):
        half = TILE // 2
        first = bias_ref[h, pl.ds(r0, chunk), t * TILE : t * TILE + half]
        first = first + q_buf[pl.ds(r0, chunk), h * half : (h + 1) * half]
        second = bias_ref[h, pl.ds(r0, chunk), t * TILE + half : (t + 1) * TILE]
        left = jnp.concatenate([first, second], axis=1)
        return jnp.dot(left, right[h, t], preferred_element_type=f32)

    def finish(r0):
        mixed = jnp.dot(probs[...], vext[...], preferred_element_type=f32)
        width = heads * head_dim
        gated = mixed[:, :width] / mixed[:, width:]
        gated = (gated * gate_buf[pl.ds(r0, chunk), :].astype(f32)).astype(bf16)
        out_ref[0, pl.ds(r0, chunk), :] = jnp.dot(
            gated, wo_ref[...], preferred_element_type=f32
        ).astype(bf16)

    @pl.when(safe)
    def _():
        @pl.loop(0, crop // chunk)
        def _(c):
            r0 = pl.multiple_of(c * chunk, chunk)
            for h in range(heads):
                for t in range(tiles):
                    s = scores_of(r0, h, t) * scale
                    probs[:, (h * tiles + t) * TILE : (h * tiles + t + 1) * TILE] = jnp.exp2(
                        s
                    ).astype(bf16)
            finish(r0)

    @pl.when(jnp.logical_not(safe))
    def _():
        ones = jnp.ones((chunk, heads * head_dim), bf16)

        @pl.loop(0, crop // chunk)
        def _(c):
            r0 = pl.multiple_of(c * chunk, chunk)
            for h in range(heads):
                held = []
                for t in range(tiles):
                    s = scores_of(r0, h, t) * scale
                    on = lax.dot_general(
                        ones,
                        kept[t * TILE : (t + 1) * TILE, :],
                        nt,
                        preferred_element_type=f32,
                    )
                    held.append(jnp.where(on > 0.0, s, -BIG))
                most = held[0].max(axis=1, keepdims=True)
                for t in range(1, tiles):
                    most = jnp.maximum(most, held[t].max(axis=1, keepdims=True))
                for t in range(tiles):
                    probs[:, (h * tiles + t) * TILE : (h * tiles + t + 1) * TILE] = jnp.exp2(
                        held[t] - most
                    ).astype(bf16)
            finish(r0)


def attend(x_cols, col_valid, gain, nbias, w_query, w_key, w_value, w_gate, gate_bias, w_out, bias_ext, kmask, live, heads):
    cols, crop, channels = x_cols.shape
    width = w_query.shape[1]
    head_dim = width // heads
    slots = bias_ext.shape[2]
    tiles = slots // TILE
    half = TILE // 2
    chunk = 160 if crop % 160 == 0 else crop
    wq_pad = jnp.pad(
        w_query.reshape(channels, heads, head_dim), ((0, 0), (0, 0), (0, half - head_dim))
    ).reshape(channels, heads * half)
    whole = lambda a: pl.BlockSpec(a.shape, lambda j, *_: (0,) * a.ndim)
    operands = (
        x_cols,
        gain.reshape(1, -1),
        nbias.reshape(1, -1),
        wq_pad,
        w_query.T,
        w_key.T,
        w_value,
        w_gate,
        gate_bias.reshape(1, -1),
        w_out,
        bias_ext,
        kmask,
        live,
    )
    specs = [pl.BlockSpec((1, crop, channels), lambda j, *_: (j, 0, 0))]
    specs += [whole(a) for a in operands[1:]]
    return pl.pallas_call(
        functools.partial(attend_kernel, heads, head_dim, head_dim ** (-0.5), chunk),
        out_shape=jax.ShapeDtypeStruct((cols, crop, w_out.shape[1]), jnp.bfloat16),
        grid_spec=pltpu.PrefetchScalarGridSpec(
            num_scalar_prefetch=1,
            grid=(cols,),
            in_specs=specs,
            out_specs=pl.BlockSpec((1, crop, w_out.shape[1]), lambda j, *_: (j, 0, 0)),
            scratch_shapes=[
                pltpu.VMEM((slots, channels), jnp.bfloat16),
                pltpu.VMEM((crop, heads * half), jnp.bfloat16),
                pltpu.VMEM((crop, width), jnp.bfloat16),
                pltpu.VMEM((heads, tiles, TILE, TILE), jnp.bfloat16),
                pltpu.VMEM((heads * slots, 2 * width), jnp.bfloat16),
                pltpu.VMEM((chunk, heads * slots), jnp.bfloat16),
                pltpu.SMEM((1,), jnp.float32),
            ],
        ),
        compiler_params=pltpu.CompilerParams(vmem_limit_bytes=48 * 1024 * 1024),
    )(col_valid, *operands)


def local(
    pair_rep,
    token_mask,
    norm_gain,
    norm_bias,
    w_query,
    w_key,
    w_value,
    w_gate,
    gate_bias,
    w_bias,
    w_out,
):
    rows, crop, channels = pair_rep.shape
    heads = w_bias.shape[1]
    head_dim = w_query.shape[1] // heads
    per = TILE - head_dim
    tiles = -(-crop // per)

    x_cols = lax.all_to_all(pair_rep, "dap", split_axis=1, concat_axis=0, tiled=True)
    x_cols = jnp.transpose(x_cols, (1, 0, 2))

    normed = normalize(pair_rep, norm_gain, norm_bias)
    bias_proj = jnp.dot(normed, w_bias, preferred_element_type=jnp.float32).astype(jnp.bfloat16)
    bias_full = lax.all_gather(jnp.transpose(bias_proj, (0, 2, 1)), "dap", axis=0, tiled=True)
    bias_full = jnp.transpose(bias_full, (1, 2, 0))
    bias_ext = jnp.pad(bias_full, ((0, 0), (0, 0), (0, tiles * per - crop)))
    bias_ext = bias_ext.reshape(heads, crop, tiles, per)
    bias_ext = jnp.pad(bias_ext, ((0, 0), (0, 0), (0, 0), (head_dim, 0)))
    bias_ext = bias_ext.reshape(heads, crop, tiles * TILE)

    def slotted(v):
        v = jnp.pad(v, (0, tiles * per - crop)).reshape(tiles, per)
        v = jnp.pad(v, ((0, 0), (0, TILE - per))).reshape(-1)
        return jnp.broadcast_to(v[:, None], (tiles * TILE, w_query.shape[1])).astype(jnp.bfloat16)

    offset = lax.axis_index("dap") * rows
    col_valid = lax.dynamic_slice_in_dim(token_mask, offset, rows)
    out_cols = attend(
        x_cols, col_valid, norm_gain, norm_bias, w_query, w_key, w_value, w_gate, gate_bias, w_out,
        bias_ext, slotted(token_mask), slotted(jnp.ones_like(token_mask)), heads,
    )
    return lax.all_to_all(
        jnp.transpose(out_cols, (1, 0, 2)), "dap", split_axis=0, concat_axis=1, tiled=True
    )


def solution(mesh):
    return jax.shard_map(
        local,
        mesh=mesh,
        in_specs=(
            P(("rep", "dap"), None, None),
            P("rep"),
            P(),
            P(),
            P(),
            P(),
            P(),
            P(),
            P(),
            P(),
            P(),
        ),
        out_specs=P(("rep", "dap"), None, None),
        check_vma=False,
    )
```

```python
import functools

import jax
import jax.numpy as jnp
from jax import lax
from jax.experimental import pallas as pl
from jax.experimental.pallas import tpu as pltpu
from jax.sharding import PartitionSpec as P

LOG2E = 1.4426950408889634
TILE = 256
SAFE = 70.0
BIG = 1e30


def normalize(block, norm_gain, norm_bias):
    widened = block.astype(jnp.float32)
    average = jnp.mean(widened, axis=-1, keepdims=True)
    centred = widened - average
    variance = jnp.mean(centred * centred, axis=-1, keepdims=True)
    return (centred * lax.rsqrt(variance + 1e-05) * norm_gain + norm_bias).astype(jnp.bfloat16)


def attend_kernel(
    heads,
    head_dim,
    q_scale,
    chunk,
    mask_ref,
    x_ref,
    gain_ref,
    nbias_ref,
    wq_ref,
    wqt_ref,
    wkt_ref,
    wv_ref,
    wg_ref,
    gbias_ref,
    wo_ref,
    bias_ref,
    kmask_ref,
    live_ref,
    out_ref,
    npad,
    q_buf,
    gate_buf,
    right,
    vext,
    probs,
    top_bias,
):
    step = pl.program_id(0)
    crop = x_ref.shape[1]
    slots = npad.shape[0]
    tiles = slots // TILE
    per = TILE - head_dim
    f32, bf16 = jnp.float32, jnp.bfloat16

    @pl.when(step == 0)
    def _():
        npad[...] = jnp.zeros_like(npad)
        r = lax.broadcasted_iota(jnp.int32, (TILE, TILE), 0)
        n = lax.broadcasted_iota(jnp.int32, (TILE, TILE), 1)
        eye = jnp.where(r == n + head_dim, 1.0, 0.0).astype(bf16)
        for h in range(heads):
            for t in range(tiles):
                right[h, t] = eye
        largest = jnp.zeros((16, slots), bf16)
        for h in range(heads):
            for r in range(0, crop, 16):
                largest = jnp.maximum(largest, jnp.abs(bias_ref[h, r : r + 16, :]))
        top_bias[0] = jnp.max(largest.astype(f32))

    normed = normalize(x_ref[0], gain_ref[...], nbias_ref[...])
    for t in range(tiles):
        count = min(per, crop - t * per)
        npad[t * TILE : t * TILE + count, :] = normed[t * per : t * per + count, :]
    q_buf[...] = (
        jnp.dot(normed, wq_ref[...], preferred_element_type=f32) * q_scale
    ).astype(bf16)
    gate_buf[...] = jax.nn.sigmoid(
        jnp.dot(normed, wg_ref[...], preferred_element_type=f32) + gbias_ref[...]
    ).astype(bf16)
    nt = (((1,), (1,)), ((), ()))
    padded = npad[...]
    key_t = lax.dot_general(wkt_ref[...], padded, nt, preferred_element_type=f32).astype(bf16)
    query_t = (
        lax.dot_general(wqt_ref[...], normed, nt, preferred_element_type=f32) * q_scale
    ).astype(bf16)
    value = jnp.dot(padded, wv_ref[...], preferred_element_type=f32).astype(bf16)

    bound = jnp.zeros((1, 1), f32)
    lanes = lax.broadcasted_iota(jnp.int32, (slots, heads * head_dim), 1)
    col_on = mask_ref[step] > 0
    kept = jnp.where(col_on, kmask_ref[...].astype(f32), live_ref[...].astype(f32)).astype(bf16)
    zero = jnp.zeros_like(kept)
    value = value * kept
    for h in range(heads):
        rows = slice(h * head_dim, (h + 1) * head_dim)
        k_h = key_t[rows, :]
        q_h = query_t[rows, :]
        for t in range(tiles):
            right[h, t, 0:head_dim, :] = k_h[:, t * TILE : (t + 1) * TILE]
        k2 = jnp.max(
            jnp.sum(jnp.square(k_h.astype(f32)), axis=0, keepdims=True), axis=1, keepdims=True
        )
        q2 = jnp.max(
            jnp.sum(jnp.square(q_h.astype(f32)), axis=0, keepdims=True), axis=1, keepdims=True
        )
        bound = jnp.maximum(bound, k2 * q2)
        mine = (lanes >= h * head_dim) & (lanes < (h + 1) * head_dim)
        vext[h * slots : (h + 1) * slots, 0 : heads * head_dim] = jnp.where(mine, value, zero)
        vext[h * slots : (h + 1) * slots, heads * head_dim : 2 * heads * head_dim] = jnp.where(
            mine, kept, zero
        )
    bound = jnp.sqrt(bound[0, 0]) + top_bias[0]
    safe = bound < SAFE
    scale = jnp.where(col_on, LOG2E, 0.0)

    def scores_of(r0, h, t):
        half = TILE // 2
        first = bias_ref[h, pl.ds(r0, chunk), t * TILE : t * TILE + half]
        first = first + q_buf[pl.ds(r0, chunk), h * half : (h + 1) * half]
        second = bias_ref[h, pl.ds(r0, chunk), t * TILE + half : (t + 1) * TILE]
        left = jnp.concatenate([first, second], axis=1)
        return jnp.dot(left, right[h, t], preferred_element_type=f32)

    def finish(r0):
        mixed = jnp.dot(probs[...], vext[...], preferred_element_type=f32)
        width = heads * head_dim
        gated = mixed[:, :width] / mixed[:, width:]
        gated = (gated * gate_buf[pl.ds(r0, chunk), :].astype(f32)).astype(bf16)
        out_ref[0, pl.ds(r0, chunk), :] = jnp.dot(
            gated, wo_ref[...], preferred_element_type=f32
        ).astype(bf16)

    @pl.when(safe)
    def _():
        @pl.loop(0, crop // chunk)
        def _(c):
            r0 = pl.multiple_of(c * chunk, chunk)
            for h in range(heads):
                for t in range(tiles):
                    s = scores_of(r0, h, t) * scale
                    probs[:, (h * tiles + t) * TILE : (h * tiles + t + 1) * TILE] = jnp.exp2(
                        s
                    ).astype(bf16)
            finish(r0)

    @pl.when(jnp.logical_not(safe))
    def _():
        ones = jnp.ones((chunk, heads * head_dim), bf16)

        @pl.loop(0, crop // chunk)
        def _(c):
            r0 = pl.multiple_of(c * chunk, chunk)
            for h in range(heads):
                held = []
                for t in range(tiles):
                    s = scores_of(r0, h, t) * scale
                    on = lax.dot_general(
                        ones,
                        kept[t * TILE : (t + 1) * TILE, :],
                        nt,
                        preferred_element_type=f32,
                    )
                    held.append(jnp.where(on > 0.0, s, -BIG))
                most = held[0].max(axis=1, keepdims=True)
                for t in range(1, tiles):
                    most = jnp.maximum(most, held[t].max(axis=1, keepdims=True))
                for t in range(tiles):
                    probs[:, (h * tiles + t) * TILE : (h * tiles + t + 1) * TILE] = jnp.exp2(
                        held[t] - most
                    ).astype(bf16)
            finish(r0)


def attend(x_cols, col_valid, gain, nbias, w_query, w_key, w_value, w_gate, gate_bias, w_out, bias_ext, kmask, live, heads):
    cols, crop, channels = x_cols.shape
    width = w_query.shape[1]
    head_dim = width // heads
    slots = bias_ext.shape[2]
    tiles = slots // TILE
    half = TILE // 2
    chunk = 160 if crop % 160 == 0 else crop
    wq_pad = jnp.pad(
        w_query.reshape(channels, heads, head_dim), ((0, 0), (0, 0), (0, half - head_dim))
    ).reshape(channels, heads * half)
    whole = lambda a: pl.BlockSpec(a.shape, lambda j, *_: (0,) * a.ndim)
    operands = (
        x_cols,
        gain.reshape(1, -1),
        nbias.reshape(1, -1),
        wq_pad,
        w_query.T,
        w_key.T,
        w_value,
        w_gate,
        gate_bias.reshape(1, -1),
        w_out,
        bias_ext,
        kmask,
        live,
    )
    specs = [pl.BlockSpec((1, crop, channels), lambda j, *_: (j, 0, 0))]
    specs += [whole(a) for a in operands[1:]]
    return pl.pallas_call(
        functools.partial(attend_kernel, heads, head_dim, head_dim ** (-0.5), chunk),
        out_shape=jax.ShapeDtypeStruct((cols, crop, w_out.shape[1]), jnp.bfloat16),
        grid_spec=pltpu.PrefetchScalarGridSpec(
            num_scalar_prefetch=1,
            grid=(cols,),
            in_specs=specs,
            out_specs=pl.BlockSpec((1, crop, w_out.shape[1]), lambda j, *_: (j, 0, 0)),
            scratch_shapes=[
                pltpu.VMEM((slots, channels), jnp.bfloat16),
                pltpu.VMEM((crop, heads * half), jnp.bfloat16),
                pltpu.VMEM((crop, width), jnp.bfloat16),
                pltpu.VMEM((heads, tiles, TILE, TILE), jnp.bfloat16),
                pltpu.VMEM((heads * slots, 2 * width), jnp.bfloat16),
                pltpu.VMEM((chunk, heads * slots), jnp.bfloat16),
                pltpu.SMEM((1,), jnp.float32),
            ],
        ),
        cost_estimate=pl.CostEstimate(
            flops=cols * 5_800_000_000,
            bytes_accessed=2 * cols * crop * channels * 2,
            transcendentals=0,
        ),
        compiler_params=pltpu.CompilerParams(vmem_limit_bytes=48 * 1024 * 1024),
    )(col_valid, *operands)


def local(
    pair_rep,
    token_mask,
    norm_gain,
    norm_bias,
    w_query,
    w_key,
    w_value,
    w_gate,
    gate_bias,
    w_bias,
    w_out,
):
    rows, crop, channels = pair_rep.shape
    heads = w_bias.shape[1]
    head_dim = w_query.shape[1] // heads
    per = TILE - head_dim
    tiles = -(-crop // per)

    group = 4 if rows % 4 == 0 else rows
    count = rows // group
    devices = crop // rows
    sent = pair_rep.reshape(rows, devices, count, group, channels)
    sent = jnp.transpose(sent, (2, 1, 3, 0, 4)).reshape(count, devices, group * rows, channels)
    arrived = [
        lax.all_to_all(sent[c], "dap", split_axis=0, concat_axis=0, tiled=True)
        for c in range(count)
    ]

    normed = normalize(pair_rep, norm_gain, norm_bias)
    bias_proj = jnp.dot(normed, w_bias, preferred_element_type=jnp.float32).astype(jnp.bfloat16)
    bias_full = lax.all_gather(jnp.transpose(bias_proj, (0, 2, 1)), "dap", axis=0, tiled=True)
    bias_full = jnp.transpose(bias_full, (1, 2, 0))
    bias_ext = jnp.pad(bias_full, ((0, 0), (0, 0), (0, tiles * per - crop)))
    bias_ext = bias_ext.reshape(heads, crop, tiles, per)
    bias_ext = jnp.pad(bias_ext, ((0, 0), (0, 0), (0, 0), (head_dim, 0)))
    bias_ext = bias_ext.reshape(heads, crop, tiles * TILE)

    def slotted(v):
        v = jnp.pad(v, (0, tiles * per - crop)).reshape(tiles, per)
        v = jnp.pad(v, ((0, 0), (0, TILE - per))).reshape(-1)
        return jnp.broadcast_to(v[:, None], (tiles * TILE, w_query.shape[1])).astype(jnp.bfloat16)

    offset = lax.axis_index("dap") * rows
    col_valid = lax.dynamic_slice_in_dim(token_mask, offset, rows)
    kmask, live = slotted(token_mask), slotted(jnp.ones_like(token_mask))
    returned = []
    for c in range(count):
        x_cols = arrived[c].reshape(devices, group, rows, channels)
        x_cols = jnp.transpose(x_cols, (1, 0, 2, 3)).reshape(group, crop, channels)
        out_cols = attend(
            x_cols, col_valid[c * group : (c + 1) * group], norm_gain, norm_bias, w_query, w_key,
            w_value, w_gate, gate_bias, w_out, bias_ext, kmask, live, heads,
        )
        out_cols = out_cols.reshape(group, devices, rows, channels)
        out_cols = jnp.transpose(out_cols, (1, 0, 2, 3)).reshape(devices, group * rows, channels)
        returned.append(
            lax.all_to_all(out_cols, "dap", split_axis=0, concat_axis=0, tiled=True)
        )
    update = jnp.stack(returned).reshape(count, devices, group, rows, channels)
    return jnp.transpose(update, (3, 1, 0, 2, 4)).reshape(rows, crop, channels)


def solution(mesh):
    return jax.shard_map(
        local,
        mesh=mesh,
        in_specs=(
            P(("rep", "dap"), None, None),
            P("rep"),
            P(),
            P(),
            P(),
            P(),
            P(),
            P(),
            P(),
            P(),
            P(),
        ),
        out_specs=P(("rep", "dap"), None, None),
        check_vma=False,
    )
```

```python
import functools

import jax
import jax.numpy as jnp
from jax import lax
from jax.experimental import pallas as pl
from jax.experimental.pallas import tpu as pltpu
from jax.sharding import PartitionSpec as P

LOG2E = 1.4426950408889634
TILE = 256
SAFE = 70.0
BIG = 1e30
CHUNK = 640


def normalize(block, norm_gain, norm_bias):
    widened = block.astype(jnp.float32)
    average = jnp.mean(widened, axis=-1, keepdims=True)
    centred = widened - average
    variance = jnp.mean(centred * centred, axis=-1, keepdims=True)
    return (centred * lax.rsqrt(variance + 1e-05) * norm_gain + norm_bias).astype(jnp.bfloat16)


def attend_kernel(
    heads,
    head_dim,
    q_scale,
    chunk,
    mask_ref,
    x_ref,
    gain_ref,
    nbias_ref,
    wq_ref,
    wqt_ref,
    wkt_ref,
    wv_ref,
    wg_ref,
    gbias_ref,
    wo_ref,
    bias_ref,
    kmask_ref,
    live_ref,
    out_ref,
    npad,
    q_buf,
    gate_buf,
    right,
    vext,
    probs,
    top_bias,
):
    step = pl.program_id(0)
    crop = x_ref.shape[1]
    slots = npad.shape[0]
    tiles = slots // TILE
    per = TILE - head_dim
    f32, bf16 = jnp.float32, jnp.bfloat16

    @pl.when(step == 0)
    def _():
        npad[...] = jnp.zeros_like(npad)
        r = lax.broadcasted_iota(jnp.int32, (TILE, TILE), 0)
        n = lax.broadcasted_iota(jnp.int32, (TILE, TILE), 1)
        eye = jnp.where(r == n + head_dim, 1.0, 0.0).astype(bf16)
        for h in range(heads):
            for t in range(tiles):
                right[h, t] = eye
        largest = jnp.zeros((16, slots), bf16)
        for h in range(heads):
            for r in range(0, crop, 16):
                largest = jnp.maximum(largest, jnp.abs(bias_ref[h, r : r + 16, :]))
        top_bias[0] = jnp.max(largest.astype(f32))

    normed = normalize(x_ref[0], gain_ref[...], nbias_ref[...])
    for t in range(tiles):
        count = min(per, crop - t * per)
        npad[t * TILE : t * TILE + count, :] = normed[t * per : t * per + count, :]
    q_buf[...] = (
        jnp.dot(normed, wq_ref[...], preferred_element_type=f32) * q_scale
    ).astype(bf16)
    gate_buf[...] = jax.nn.sigmoid(
        jnp.dot(normed, wg_ref[...], preferred_element_type=f32) + gbias_ref[...]
    ).astype(bf16)
    nt = (((1,), (1,)), ((), ()))
    padded = npad[...]
    key_t = lax.dot_general(wkt_ref[...], padded, nt, preferred_element_type=f32).astype(bf16)
    query_t = (
        lax.dot_general(wqt_ref[...], normed, nt, preferred_element_type=f32) * q_scale
    ).astype(bf16)
    value = jnp.dot(padded, wv_ref[...], preferred_element_type=f32).astype(bf16)

    bound = jnp.zeros((1, 1), f32)
    lanes = lax.broadcasted_iota(jnp.int32, (slots, heads * head_dim), 1)
    col_on = mask_ref[step] > 0
    kept = jnp.where(col_on, kmask_ref[...].astype(f32), live_ref[...].astype(f32)).astype(bf16)
    zero = jnp.zeros_like(kept)
    value = value * kept
    for h in range(heads):
        rows = slice(h * head_dim, (h + 1) * head_dim)
        k_h = key_t[rows, :]
        q_h = query_t[rows, :]
        for t in range(tiles):
            right[h, t, 0:head_dim, :] = k_h[:, t * TILE : (t + 1) * TILE]
        k2 = jnp.max(
            jnp.sum(jnp.square(k_h.astype(f32)), axis=0, keepdims=True), axis=1, keepdims=True
        )
        q2 = jnp.max(
            jnp.sum(jnp.square(q_h.astype(f32)), axis=0, keepdims=True), axis=1, keepdims=True
        )
        bound = jnp.maximum(bound, k2 * q2)
        mine = (lanes >= h * head_dim) & (lanes < (h + 1) * head_dim)
        vext[h * slots : (h + 1) * slots, 0 : heads * head_dim] = jnp.where(mine, value, zero)
        vext[h * slots : (h + 1) * slots, heads * head_dim : 2 * heads * head_dim] = jnp.where(
            mine, kept, zero
        )
    bound = jnp.sqrt(bound[0, 0]) + top_bias[0]
    safe = bound < SAFE
    scale = jnp.where(col_on, LOG2E, 0.0)

    def scores_of(r0, h, t):
        half = TILE // 2
        first = bias_ref[h, pl.ds(r0, chunk), t * TILE : t * TILE + half]
        first = first + q_buf[pl.ds(r0, chunk), h * half : (h + 1) * half]
        second = bias_ref[h, pl.ds(r0, chunk), t * TILE + half : (t + 1) * TILE]
        left = jnp.concatenate([first, second], axis=1)
        return jnp.dot(left, right[h, t], preferred_element_type=f32)

    def finish(r0):
        mixed = jnp.dot(probs[...], vext[...], preferred_element_type=f32)
        width = heads * head_dim
        gated = mixed[:, :width] / mixed[:, width:]
        gated = (gated * gate_buf[pl.ds(r0, chunk), :].astype(f32)).astype(bf16)
        out_ref[0, pl.ds(r0, chunk), :] = jnp.dot(
            gated, wo_ref[...], preferred_element_type=f32
        ).astype(bf16)

    @pl.when(safe)
    def _():
        @pl.loop(0, crop // chunk)
        def _(c):
            r0 = pl.multiple_of(c * chunk, chunk)
            for h in range(heads):
                for t in range(tiles):
                    s = scores_of(r0, h, t) * scale
                    probs[:, (h * tiles + t) * TILE : (h * tiles + t + 1) * TILE] = jnp.exp2(
                        s
                    ).astype(bf16)
            finish(r0)

    @pl.when(jnp.logical_not(safe))
    def _():
        ones = jnp.ones((chunk, heads * head_dim), bf16)

        @pl.loop(0, crop // chunk)
        def _(c):
            r0 = pl.multiple_of(c * chunk, chunk)
            for h in range(heads):
                held = []
                for t in range(tiles):
                    s = scores_of(r0, h, t) * scale
                    on = lax.dot_general(
                        ones,
                        kept[t * TILE : (t + 1) * TILE, :],
                        nt,
                        preferred_element_type=f32,
                    )
                    held.append(jnp.where(on > 0.0, s, -BIG))
                most = held[0].max(axis=1, keepdims=True)
                for t in range(1, tiles):
                    most = jnp.maximum(most, held[t].max(axis=1, keepdims=True))
                for t in range(tiles):
                    probs[:, (h * tiles + t) * TILE : (h * tiles + t + 1) * TILE] = jnp.exp2(
                        held[t] - most
                    ).astype(bf16)
            finish(r0)


def attend(x_cols, col_valid, gain, nbias, w_query, w_key, w_value, w_gate, gate_bias, w_out, bias_ext, kmask, live, heads):
    cols, crop, channels = x_cols.shape
    width = w_query.shape[1]
    head_dim = width // heads
    slots = bias_ext.shape[2]
    tiles = slots // TILE
    half = TILE // 2
    chunk = CHUNK if crop % CHUNK == 0 else crop
    wq_pad = jnp.pad(
        w_query.reshape(channels, heads, head_dim), ((0, 0), (0, 0), (0, half - head_dim))
    ).reshape(channels, heads * half)
    whole = lambda a: pl.BlockSpec(a.shape, lambda j, *_: (0,) * a.ndim)
    operands = (
        x_cols,
        gain.reshape(1, -1),
        nbias.reshape(1, -1),
        wq_pad,
        w_query.T,
        w_key.T,
        w_value,
        w_gate,
        gate_bias.reshape(1, -1),
        w_out,
        bias_ext,
        kmask,
        live,
    )
    specs = [pl.BlockSpec((1, crop, channels), lambda j, *_: (j, 0, 0))]
    specs += [whole(a) for a in operands[1:]]
    return pl.pallas_call(
        functools.partial(attend_kernel, heads, head_dim, head_dim ** (-0.5), chunk),
        out_shape=jax.ShapeDtypeStruct((cols, crop, w_out.shape[1]), jnp.bfloat16),
        grid_spec=pltpu.PrefetchScalarGridSpec(
            num_scalar_prefetch=1,
            grid=(cols,),
            in_specs=specs,
            out_specs=pl.BlockSpec((1, crop, w_out.shape[1]), lambda j, *_: (j, 0, 0)),
            scratch_shapes=[
                pltpu.VMEM((slots, channels), jnp.bfloat16),
                pltpu.VMEM((crop, heads * half), jnp.bfloat16),
                pltpu.VMEM((crop, width), jnp.bfloat16),
                pltpu.VMEM((heads, tiles, TILE, TILE), jnp.bfloat16),
                pltpu.VMEM((heads * slots, 2 * width), jnp.bfloat16),
                pltpu.VMEM((chunk, heads * slots), jnp.bfloat16),
                pltpu.SMEM((1,), jnp.float32),
            ],
        ),
        cost_estimate=pl.CostEstimate(
            flops=cols * 4_200_000_000,
            bytes_accessed=2 * cols * crop * channels * 2,
            transcendentals=0,
        ),
        compiler_params=pltpu.CompilerParams(vmem_limit_bytes=60 * 1024 * 1024),
    )(col_valid, *operands)


def local(
    pair_rep,
    token_mask,
    norm_gain,
    norm_bias,
    w_query,
    w_key,
    w_value,
    w_gate,
    gate_bias,
    w_bias,
    w_out,
):
    rows, crop, channels = pair_rep.shape
    heads = w_bias.shape[1]
    head_dim = w_query.shape[1] // heads
    per = TILE - head_dim
    tiles = -(-crop // per)

    group = 4 if rows % 4 == 0 else rows
    count = rows // group
    devices = crop // rows
    early = (3 * count + 4) // 5
    by_owner = pair_rep.reshape(rows, devices, rows, channels)

    def sent(first, last):
        part = jnp.transpose(by_owner[:, :, first * group : last * group], (1, 2, 0, 3))
        return part.reshape(devices, (last - first) * group * rows, channels)

    def exchange(block):
        return lax.all_to_all(block, "dap", split_axis=0, concat_axis=0, tiled=True)

    def columns_of(block):
        split = jnp.transpose(block.reshape(devices, -1, rows, channels), (1, 0, 2, 3))
        return split.reshape(-1, crop, channels)

    normed = normalize(pair_rep, norm_gain, norm_bias)
    bias_proj = jnp.dot(normed, w_bias, preferred_element_type=jnp.float32).astype(jnp.bfloat16)
    bias_proj = jnp.transpose(bias_proj, (0, 2, 1))
    bias_proj, sent_early = lax.optimization_barrier((bias_proj, sent(0, early)))
    bias_full = lax.all_gather(bias_proj, "dap", axis=0, tiled=True)
    arrived = exchange(sent_early)
    x_early = columns_of(arrived)
    if early < count:
        bias_full, x_early, sent_late = lax.optimization_barrier(
            (bias_full, x_early, sent(early, count))
        )
        x_late = columns_of(exchange(sent_late))
    bias_full = jnp.transpose(bias_full, (1, 2, 0))
    blank = jnp.zeros((heads, crop, head_dim), jnp.bfloat16)
    pieces = []
    for t in range(tiles):
        pieces += [blank, bias_full[:, :, t * per : min((t + 1) * per, crop)]]
    pieces.append(jnp.zeros((heads, crop, tiles * per - crop), jnp.bfloat16))
    bias_ext = jnp.concatenate(pieces, axis=2)

    def slotted(v):
        v = jnp.pad(v, (0, tiles * per - crop)).reshape(tiles, per)
        v = jnp.pad(v, ((0, 0), (0, TILE - per))).reshape(-1)
        return jnp.broadcast_to(v[:, None], (tiles * TILE, w_query.shape[1])).astype(jnp.bfloat16)

    offset = lax.axis_index("dap") * rows
    col_valid = lax.dynamic_slice_in_dim(token_mask, offset, rows)
    kmask, live = slotted(token_mask), slotted(jnp.ones_like(token_mask))
    returned = []
    for c in range(count):
        if c < early:
            x_cols = x_early[c * group : (c + 1) * group]
        else:
            x_cols = x_late[(c - early) * group : (c - early + 1) * group]
        out_cols = attend(
            x_cols, col_valid[c * group : (c + 1) * group], norm_gain, norm_bias, w_query, w_key,
            w_value, w_gate, gate_bias, w_out, bias_ext, kmask, live, heads,
        )
        out_cols = out_cols.reshape(group, devices, rows, channels)
        out_cols = jnp.transpose(out_cols, (1, 0, 2, 3)).reshape(devices, group * rows, channels)
        returned.append(exchange(out_cols))
    update = jnp.stack(returned).reshape(count, devices, group, rows, channels)
    return jnp.transpose(update, (3, 1, 0, 2, 4)).reshape(rows, crop, channels)


def solution(mesh):
    return jax.shard_map(
        local,
        mesh=mesh,
        in_specs=(
            P(("rep", "dap"), None, None),
            P("rep"),
            P(),
            P(),
            P(),
            P(),
            P(),
            P(),
            P(),
            P(),
            P(),
        ),
        out_specs=P(("rep", "dap"), None, None),
        check_vma=False,
    )
```

```python
import functools

import jax
import jax.numpy as jnp
from jax import lax
from jax.experimental import pallas as pl
from jax.experimental.pallas import tpu as pltpu
from jax.sharding import PartitionSpec as P

LOG2E = 1.4426950408889634
TILE = 256
SAFE = 70.0
BIG = 1e30
CHUNK = 640


def normalize(block, norm_gain, norm_bias):
    widened = block.astype(jnp.float32)
    average = jnp.mean(widened, axis=-1, keepdims=True)
    centred = widened - average
    variance = jnp.mean(centred * centred, axis=-1, keepdims=True)
    return (centred * lax.rsqrt(variance + 1e-05) * norm_gain + norm_bias).astype(jnp.bfloat16)


def attend_kernel(
    heads,
    head_dim,
    q_scale,
    chunk,
    mask_ref,
    x_ref,
    gain_ref,
    nbias_ref,
    wq_ref,
    wqt_ref,
    wkt_ref,
    wv_ref,
    wg_ref,
    gbias_ref,
    wo_ref,
    bias_ref,
    kmask_ref,
    live_ref,
    out_ref,
    npad,
    q_buf,
    gate_buf,
    right,
    vext,
    probs,
    top_bias,
):
    step = pl.program_id(0)
    crop = x_ref.shape[1]
    slots = npad.shape[0]
    tiles = slots // TILE
    per = TILE - head_dim
    f32, bf16 = jnp.float32, jnp.bfloat16

    @pl.when(step == 0)
    def _():
        npad[...] = jnp.zeros_like(npad)
        r = lax.broadcasted_iota(jnp.int32, (TILE, TILE), 0)
        n = lax.broadcasted_iota(jnp.int32, (TILE, TILE), 1)
        eye = jnp.where(r == n + head_dim, 1.0, 0.0).astype(bf16)
        for h in range(heads):
            for t in range(tiles):
                right[h, t] = eye
        largest = jnp.zeros((16, slots), bf16)
        for h in range(heads):
            for r in range(0, crop, 16):
                largest = jnp.maximum(largest, jnp.abs(bias_ref[h, r : r + 16, :]))
        top_bias[0] = jnp.max(largest.astype(f32))

    normed = normalize(x_ref[0], gain_ref[...], nbias_ref[...])
    for t in range(tiles):
        count = min(per, crop - t * per)
        npad[t * TILE : t * TILE + count, :] = normed[t * per : t * per + count, :]
    q_buf[...] = (
        jnp.dot(normed, wq_ref[...], preferred_element_type=f32) * q_scale
    ).astype(bf16)
    gate_buf[...] = jax.nn.sigmoid(
        jnp.dot(normed, wg_ref[...], preferred_element_type=f32) + gbias_ref[...]
    ).astype(bf16)
    nt = (((1,), (1,)), ((), ()))
    padded = npad[...]
    key_t = lax.dot_general(wkt_ref[...], padded, nt, preferred_element_type=f32).astype(bf16)
    query_t = (
        lax.dot_general(wqt_ref[...], normed, nt, preferred_element_type=f32) * q_scale
    ).astype(bf16)
    value = jnp.dot(padded, wv_ref[...], preferred_element_type=f32).astype(bf16)

    bound = jnp.zeros((1, 1), f32)
    lanes = lax.broadcasted_iota(jnp.int32, (slots, heads * head_dim), 1)
    col_on = mask_ref[step] > 0
    kept = jnp.where(col_on, kmask_ref[...].astype(f32), live_ref[...].astype(f32)).astype(bf16)
    zero = jnp.zeros_like(kept)
    value = value * kept
    for h in range(heads):
        rows = slice(h * head_dim, (h + 1) * head_dim)
        k_h = key_t[rows, :]
        q_h = query_t[rows, :]
        for t in range(tiles):
            right[h, t, 0:head_dim, :] = k_h[:, t * TILE : (t + 1) * TILE]
        k2 = jnp.max(
            jnp.sum(jnp.square(k_h.astype(f32)), axis=0, keepdims=True), axis=1, keepdims=True
        )
        q2 = jnp.max(
            jnp.sum(jnp.square(q_h.astype(f32)), axis=0, keepdims=True), axis=1, keepdims=True
        )
        bound = jnp.maximum(bound, k2 * q2)
        mine = (lanes >= h * head_dim) & (lanes < (h + 1) * head_dim)
        vext[h * slots : (h + 1) * slots, 0 : heads * head_dim] = jnp.where(mine, value, zero)
        vext[h * slots : (h + 1) * slots, heads * head_dim : 2 * heads * head_dim] = jnp.where(
            mine, kept, zero
        )
    bound = jnp.sqrt(bound[0, 0]) + top_bias[0]
    safe = bound < SAFE
    scale = jnp.where(col_on, LOG2E, 0.0)

    def scores_of(r0, h, t):
        half = TILE // 2
        first = bias_ref[h, pl.ds(r0, chunk), t * TILE : t * TILE + half]
        first = first + q_buf[pl.ds(r0, chunk), h * half : (h + 1) * half]
        second = bias_ref[h, pl.ds(r0, chunk), t * TILE + half : (t + 1) * TILE]
        left = jnp.concatenate([first, second], axis=1)
        return jnp.dot(left, right[h, t], preferred_element_type=f32)

    def finish(r0):
        mixed = jnp.dot(probs[...], vext[...], preferred_element_type=f32)
        width = heads * head_dim
        gated = mixed[:, :width] / mixed[:, width:]
        gated = (gated * gate_buf[pl.ds(r0, chunk), :].astype(f32)).astype(bf16)
        out_ref[0, pl.ds(r0, chunk), :] = jnp.dot(
            gated, wo_ref[...], preferred_element_type=f32
        ).astype(bf16)

    @pl.when(safe)
    def _():
        @pl.loop(0, crop // chunk)
        def _(c):
            r0 = pl.multiple_of(c * chunk, chunk)
            for h in range(heads):
                for t in range(tiles):
                    s = scores_of(r0, h, t) * scale
                    probs[:, (h * tiles + t) * TILE : (h * tiles + t + 1) * TILE] = jnp.exp2(
                        s
                    ).astype(bf16)
            finish(r0)

    @pl.when(jnp.logical_not(safe))
    def _():
        ones = jnp.ones((chunk, heads * head_dim), bf16)

        @pl.loop(0, crop // chunk)
        def _(c):
            r0 = pl.multiple_of(c * chunk, chunk)
            for h in range(heads):
                held = []
                for t in range(tiles):
                    s = scores_of(r0, h, t) * scale
                    on = lax.dot_general(
                        ones,
                        kept[t * TILE : (t + 1) * TILE, :],
                        nt,
                        preferred_element_type=f32,
                    )
                    held.append(jnp.where(on > 0.0, s, -BIG))
                most = held[0].max(axis=1, keepdims=True)
                for t in range(1, tiles):
                    most = jnp.maximum(most, held[t].max(axis=1, keepdims=True))
                for t in range(tiles):
                    probs[:, (h * tiles + t) * TILE : (h * tiles + t + 1) * TILE] = jnp.exp2(
                        held[t] - most
                    ).astype(bf16)
            finish(r0)


def slot_kernel(head_dim, src_ref, out_ref, laid):
    crop = src_ref.shape[0]
    slots = laid.shape[0]
    per = TILE - head_dim
    laid[...] = jnp.zeros_like(laid)
    for t in range(slots // TILE):
        count = min(per, crop - t * per)
        at = t * TILE + head_dim
        laid[at : at + count, :] = src_ref[t * per : t * per + count, :]
    out_ref[0] = laid[...].T


def slot_bias(bias_rows, heads, head_dim, tiles):
    crop = bias_rows.shape[0]
    slots = tiles * TILE
    return pl.pallas_call(
        functools.partial(slot_kernel, head_dim),
        out_shape=jax.ShapeDtypeStruct((heads, crop, slots), jnp.bfloat16),
        grid=(heads,),
        in_specs=[pl.BlockSpec((crop, crop), lambda h: (0, h))],
        out_specs=pl.BlockSpec((1, crop, slots), lambda h: (h, 0, 0)),
        scratch_shapes=[pltpu.VMEM((slots, crop), jnp.bfloat16)],
        compiler_params=pltpu.CompilerParams(vmem_limit_bytes=32 * 1024 * 1024),
    )(bias_rows)


def attend(x_cols, col_valid, gain, nbias, w_query, w_key, w_value, w_gate, gate_bias, w_out, bias_ext, kmask, live, heads):
    cols, crop, channels = x_cols.shape
    width = w_query.shape[1]
    head_dim = width // heads
    slots = bias_ext.shape[2]
    tiles = slots // TILE
    half = TILE // 2
    chunk = CHUNK if crop % CHUNK == 0 else crop
    wq_pad = jnp.pad(
        w_query.reshape(channels, heads, head_dim), ((0, 0), (0, 0), (0, half - head_dim))
    ).reshape(channels, heads * half)
    whole = lambda a: pl.BlockSpec(a.shape, lambda j, *_: (0,) * a.ndim)
    operands = (
        x_cols,
        gain.reshape(1, -1),
        nbias.reshape(1, -1),
        wq_pad,
        w_query.T,
        w_key.T,
        w_value,
        w_gate,
        gate_bias.reshape(1, -1),
        w_out,
        bias_ext,
        kmask,
        live,
    )
    specs = [pl.BlockSpec((1, crop, channels), lambda j, *_: (j, 0, 0))]
    specs += [whole(a) for a in operands[1:]]
    return pl.pallas_call(
        functools.partial(attend_kernel, heads, head_dim, head_dim ** (-0.5), chunk),
        out_shape=jax.ShapeDtypeStruct((cols, crop, w_out.shape[1]), jnp.bfloat16),
        grid_spec=pltpu.PrefetchScalarGridSpec(
            num_scalar_prefetch=1,
            grid=(cols,),
            in_specs=specs,
            out_specs=pl.BlockSpec((1, crop, w_out.shape[1]), lambda j, *_: (j, 0, 0)),
            scratch_shapes=[
                pltpu.VMEM((slots, channels), jnp.bfloat16),
                pltpu.VMEM((crop, heads * half), jnp.bfloat16),
                pltpu.VMEM((crop, width), jnp.bfloat16),
                pltpu.VMEM((heads, tiles, TILE, TILE), jnp.bfloat16),
                pltpu.VMEM((heads * slots, 2 * width), jnp.bfloat16),
                pltpu.VMEM((chunk, heads * slots), jnp.bfloat16),
                pltpu.SMEM((1,), jnp.float32),
            ],
        ),
        cost_estimate=pl.CostEstimate(
            flops=cols * 4_200_000_000,
            bytes_accessed=2 * cols * crop * channels * 2,
            transcendentals=0,
        ),
        compiler_params=pltpu.CompilerParams(vmem_limit_bytes=60 * 1024 * 1024),
    )(col_valid, *operands)


def local(
    pair_rep,
    token_mask,
    norm_gain,
    norm_bias,
    w_query,
    w_key,
    w_value,
    w_gate,
    gate_bias,
    w_bias,
    w_out,
):
    rows, crop, channels = pair_rep.shape
    heads = w_bias.shape[1]
    head_dim = w_query.shape[1] // heads
    per = TILE - head_dim
    tiles = -(-crop // per)

    group = 4 if rows % 4 == 0 else rows
    count = rows // group
    devices = crop // rows
    early = (3 * count + 4) // 5
    by_owner = pair_rep.reshape(rows, devices, rows, channels)

    def sent(first, last):
        part = jnp.transpose(by_owner[:, :, first * group : last * group], (1, 2, 0, 3))
        return part.reshape(devices, (last - first) * group * rows, channels)

    def exchange(block):
        return lax.all_to_all(block, "dap", split_axis=0, concat_axis=0, tiled=True)

    def columns_of(block):
        split = jnp.transpose(block.reshape(devices, -1, rows, channels), (1, 0, 2, 3))
        return split.reshape(-1, crop, channels)

    normed = normalize(pair_rep, norm_gain, norm_bias)
    bias_proj = jnp.dot(normed, w_bias, preferred_element_type=jnp.float32).astype(jnp.bfloat16)
    bias_proj = jnp.transpose(bias_proj, (0, 2, 1)).reshape(rows, heads * crop)
    bias_proj, sent_early = lax.optimization_barrier((bias_proj, sent(0, early)))
    bias_full = lax.all_gather(bias_proj, "dap", axis=0, tiled=True)
    arrived = exchange(sent_early)
    x_early = columns_of(arrived)
    if early < count:
        bias_full, x_early, sent_late = lax.optimization_barrier(
            (bias_full, x_early, sent(early, count))
        )
        x_late = columns_of(exchange(sent_late))
    bias_ext = slot_bias(bias_full, heads, head_dim, tiles)

    def slotted(v):
        v = jnp.pad(v, (0, tiles * per - crop)).reshape(tiles, per)
        v = jnp.pad(v, ((0, 0), (0, TILE - per))).reshape(-1)
        return jnp.broadcast_to(v[:, None], (tiles * TILE, w_query.shape[1])).astype(jnp.bfloat16)

    offset = lax.axis_index("dap") * rows
    col_valid = lax.dynamic_slice_in_dim(token_mask, offset, rows)
    kmask, live = slotted(token_mask), slotted(jnp.ones_like(token_mask))
    returned = []
    for c in range(count):
        if c < early:
            x_cols = x_early[c * group : (c + 1) * group]
        else:
            x_cols = x_late[(c - early) * group : (c - early + 1) * group]
        out_cols = attend(
            x_cols, col_valid[c * group : (c + 1) * group], norm_gain, norm_bias, w_query, w_key,
            w_value, w_gate, gate_bias, w_out, bias_ext, kmask, live, heads,
        )
        out_cols = out_cols.reshape(group, devices, rows, channels)
        out_cols = jnp.transpose(out_cols, (1, 0, 2, 3)).reshape(devices, group * rows, channels)
        if c == 0 and early < count:
            out_cols, x_late = lax.optimization_barrier((out_cols, x_late))
        returned.append(exchange(out_cols))
    update = jnp.stack(returned).reshape(count, devices, group, rows, channels)
    return jnp.transpose(update, (3, 1, 0, 2, 4)).reshape(rows, crop, channels)


def solution(mesh):
    return jax.shard_map(
        local,
        mesh=mesh,
        in_specs=(
            P(("rep", "dap"), None, None),
            P("rep"),
            P(),
            P(),
            P(),
            P(),
            P(),
            P(),
            P(),
            P(),
            P(),
        ),
        out_specs=P(("rep", "dap"), None, None),
        check_vma=False,
    )
```
